32 devices in a mesh: parts: 2 (over y), sector: 16 (over z, x, core).
Axes of the slice: x: 2, y: 2, z: 4, core: 2. Of those that a mesh axis runs over, the one named last changes fastest.
Arguments:
- vectors: bfloat16 [2, 32, 256, 256], P(None, ('parts', 'sector')), parts along dimension 1, may hold values from -6 to 6
- left_environment_blocks: bfloat16 [32, 26, 256, 256], P(('parts', 'sector')), parts along dimension 0, may hold values from -0.375 to 0.375
- right_env: bfloat16 [32, 26, 256, 256], P(('parts', 'sector')), parts along dimension 0, may hold values from -0.078125 to 0.078125
- mpo_coef: float32 [52, 26], P('parts'), parts along dimension 0, may hold values from -6 to 6
- mpo_pattern: int32 [52, 26], P('parts'), parts along dimension 0, may hold values 0 or 1
- left_sizes: int32 [32], P('parts'), parts along dimension 0, may hold values from 64 to 256, as said below
- right_sizes: int32 [32], P('parts'), parts along dimension 0, may hold values from 64 to 256, as said below
Outputs:
- product: bfloat16 [2, 32, 256, 256], P(None, ('parts', 'sector')), parts along dimension 1
- subspace: float32 [4, 2], P('parts'), parts along dimension 0
The draws below stay inside these ranges and needn't reach their ends.
There are 2 independent parts, one for each index of `parts`. The reference program is written for one: setup_inputs(seed, part) draws one part's arguments, and reference() takes and returns one part's arrays. A program takes and returns all parts, laid end to end along the dimension named above; each array names one. Nothing has to cross between parts.
Inputs may be any that keep to these rules, and one draw needn't show every extreme that they name: `left_sizes`: at least one sector has exactly 256 states and one exactly 64. `right_sizes`: at least one sector has exactly 256 states and one exactly 64.
All inputs are finite; a program needn't handle non-finite values.
Results may differ from the reference program's by a relative error of at most 0.0064.
Values may be sent and summed in bfloat16 or wider, within the bound.
A program may use at most 128 MiB of HBM per device.

```python
import jax
import jax.numpy as jnp
from jax import lax

BLK = 256
W = 26
VEC = 2
S = 16


def sector_sizes_sample(key):
    first, second = jax.random.split(key)
    base = jax.random.randint(first, (S,), BLK // 4, BLK + 1, dtype=jnp.int32)
    order = jax.random.permutation(second, S)
    base = base.at[order[0]].set(BLK)
    base = base.at[order[1]].set(BLK // 4)
    return base


def draw_left_sizes(key, part):
    key = jax.random.fold_in(key, 11)
    return sector_sizes_sample(key)


def draw_right_sizes(key, part):
    key = jax.random.fold_in(key, 23)
    return sector_sizes_sample(key)


def touch_ends(drawn, key, least, high):
    dims = drawn.shape
    spot = [jax.random.randint(jax.random.fold_in(key, axis), (), 0, dims[axis]) for axis in range(len(dims))]
    drawn = drawn.at[tuple(spot)].set(least)
    longest = dims.index(max(dims))
    spot[longest] = (spot[longest] + 1) % dims[longest]
    return drawn.at[tuple(spot)].set(high)


def levels(key, dims, cuts, least, top_value):
    loudness = 1.0
    for dim, shards_of in cuts:
        draws = jax.random.uniform(jax.random.fold_in(jax.random.fold_in(key, 6), dim), (shards_of,), jnp.float32, least / len(cuts), top_value / len(cuts))
        loudness = loudness * jnp.repeat(jnp.exp(draws), dims[dim] // shards_of).reshape((-1,) + (1,) * (len(dims) - 1 - dim))
    return loudness


def normal_values(stream_key, shape, width, limit, pieces=(), kind=jnp.bfloat16):
    factor_of = levels(stream_key, shape, pieces, -0.22, 0.18) if pieces else 1.0
    result = jax.random.normal(stream_key, shape, jnp.float32) * width * factor_of
    return jnp.minimum(jnp.maximum(result, -limit), limit).astype(kind)


def setup_inputs(seed: int = 0, part: int = 0) -> dict:
    arg_keys = jax.random.split(jax.random.key(seed), 8)
    part_splits = jax.random.split(jax.random.fold_in(arg_keys[7], part), 8)
    vectors = normal_values(part_splits[0], (VEC, S, BLK, BLK), 1.0, 6.0, ((1, 16),))
    left_environment_blocks = normal_values(part_splits[1], (S, W, BLK, BLK), BLK ** -0.5, 0.375, ((0, 16),))
    right_env = normal_values(part_splits[2], (S, W, BLK, BLK), (W * BLK) ** -0.5, 0.078125, ((0, 16),))
    mpo_coef = normal_values(part_splits[3], (W, W), (2.0 / W ** 0.5), 6.0, (), jnp.float32)
    mpo_pattern = touch_ends((jax.random.randint(part_splits[4], (W, W), 0, 4) < 1).astype(jnp.int32), jax.random.fold_in(part_splits[4], 1), 0, 1)
    left_sizes = draw_left_sizes(jax.random.fold_in(jax.random.fold_in(arg_keys[7], part), 71), part)
    right_sizes = draw_right_sizes(jax.random.fold_in(jax.random.fold_in(arg_keys[7], part), 71), part)
    return dict(vectors=vectors, left_environment_blocks=left_environment_blocks, right_env=right_env, mpo_coef=mpo_coef, mpo_pattern=mpo_pattern, left_sizes=left_sizes, right_sizes=right_sizes)


def reference(vectors, left_environment_blocks, right_env, mpo_coef, mpo_pattern, left_sizes, right_sizes):
    coupling = mpo_coef * mpo_pattern.astype(jnp.float32)
    states = jnp.arange(BLK, dtype=jnp.int32)

    def one_sector(index):
        partner = jnp.minimum(index + 1, S - 1)
        valid = index + 1 < S
        row_ok = states < left_sizes[index]
        col_ok = (states < right_sizes[partner]) & valid
        mask = row_ok[:, None] & col_ok[None, :]
        block = lax.dynamic_index_in_dim(vectors, index, 1, keepdims=False)
        active_sector_mask = jnp.where(mask[None], block, jnp.zeros_like(block))
        left_here = left_environment_blocks[index]
        right_here = right_env[partner]
        results = []
        for vec in range(VEC):
            partial_terms = jnp.dot(left_here.reshape(W * BLK, BLK), active_sector_mask[vec], preferred_element_type=jnp.float32).reshape(W, BLK, BLK)
            mixed = jnp.einsum('wu,wac->uac', coupling, partial_terms, precision=lax.Precision.HIGHEST).astype(jnp.bfloat16)
            total = jnp.einsum('uac,udc->ad', mixed.astype(jnp.float32), right_here.astype(jnp.float32))
            total = jnp.where(mask, total, 0.0)
            results.append(total.astype(jnp.bfloat16))
        matvec_block = jnp.stack(results)
        operator_terms = jnp.einsum('hzp,ozp->ho', active_sector_mask.astype(jnp.float32), matvec_block.astype(jnp.float32))
        return (matvec_block, operator_terms)
    blocks, operator_terms = lax.map(one_sector, jnp.arange(S, dtype=jnp.int32))
    product = jnp.transpose(blocks, (1, 0, 2, 3))
    scale = 1.0 / jnp.sqrt(jnp.float32(S * BLK * BLK))
    subspace = lax.optimization_barrier(jnp.sum(operator_terms, axis=0)) * scale
    return (product, subspace)
```

```python
import functools

import jax
import jax.numpy as jnp
from jax import lax
from jax.experimental import pallas as pl
from jax.experimental.pallas import tpu as pltpu
from jax.sharding import PartitionSpec as P

MESH = pl.DeviceIdType.MESH
ROWS = 16


def kernel(
    sectors,
    group,
    left_sizes,
    right_sizes,
    coef,
    pattern,
    vectors,
    left_env,
    right_env,
    product,
    subspace,
    left,
    left_high,
    left_low,
    mixed,
    arrived,
    total,
    terms,
    gathered,
    left_sem,
    send_sem,
    recv_sem,
    term_send_sem,
    term_recv_sem,
):
    count, _, blk, _ = vectors.shape
    width = coef.shape[0]
    steps = width // group
    wide = width * ROWS
    here = lax.axis_index("sector")
    has_partner = here + 1 < sectors

    left_copy = pltpu.make_async_copy(left_env.at[0], left, left_sem)
    left_copy.start()

    barrier = pltpu.get_barrier_semaphore()

    def greet(k, carry):
        peer = lax.rem(here + k, sectors)
        pl.semaphore_signal(barrier, inc=1, device_id={"sector": peer}, device_id_type=MESH)
        return carry

    lax.fori_loop(1, sectors, greet, 0)
    pl.semaphore_wait(barrier, sectors - 1)

    def env_copy(i):
        piece = pl.ds(i * group, group)
        return pltpu.make_async_remote_copy(
            src_ref=right_env.at[0, piece],
            dst_ref=arrived.at[piece],
            send_sem=send_sem.at[i],
            recv_sem=recv_sem.at[i],
            device_id={"sector": lax.rem(here + sectors - 1, sectors)},
            device_id_type=MESH,
        )

    @pl.when(here > 0)
    def _():
        def send(i, carry):
            env_copy(i).start()
            return carry

        lax.fori_loop(0, steps, send, 0)

    partner = jnp.minimum(here + 1, sectors - 1)
    row_limit = left_sizes[here]
    col_limit = jnp.where(has_partner, right_sizes[partner], 0)
    rows = lax.broadcasted_iota(jnp.int32, (blk, blk), 0)
    cols = lax.broadcasted_iota(jnp.int32, (blk, blk), 1)
    mask = (rows < row_limit) & (cols < col_limit)
    live = [
        jnp.where(mask, vectors[v, 0].astype(jnp.float32), 0.0).astype(jnp.bfloat16)
        for v in range(count)
    ]
    live_wide = jnp.concatenate(live, axis=1)

    coupling = coef[...] * pattern[...].astype(jnp.float32)
    high = coupling.astype(jnp.bfloat16)
    low = (coupling - high.astype(jnp.float32)).astype(jnp.bfloat16)
    pick_rows = (
        lax.broadcasted_iota(jnp.int32, (wide, width), 0) // ROWS
        == lax.broadcasted_iota(jnp.int32, (wide, width), 1)
    ).astype(jnp.float32).astype(jnp.bfloat16)
    pick_cols = (
        lax.broadcasted_iota(jnp.int32, (width, wide), 1) // ROWS
        == lax.broadcasted_iota(jnp.int32, (width, wide), 0)
    ).astype(jnp.float32).astype(jnp.bfloat16)
    same = (
        lax.broadcasted_iota(jnp.int32, (wide, wide), 0) % ROWS
        == lax.broadcasted_iota(jnp.int32, (wide, wide), 1) % ROWS
    )

    def spread(part):
        tall = lax.dot_general(
            pick_rows, part, (((1,), (1,)), ((), ())), preferred_element_type=jnp.float32
        ).astype(jnp.bfloat16)
        full = jnp.dot(tall, pick_cols, preferred_element_type=jnp.float32)
        return jnp.where(same, full, 0.0).astype(jnp.bfloat16)

    spread_high = spread(high)
    spread_low = spread(low)

    left_copy.wait()

    def mix_rows(g, carry):
        piece = pl.ds(pl.multiple_of(g * ROWS, ROWS), ROWS)
        block = left[:, piece, :].reshape(wide, blk)
        out = jnp.dot(spread_high, block, preferred_element_type=jnp.float32) + jnp.dot(
            spread_low, block, preferred_element_type=jnp.float32
        )
        out_high = out.astype(jnp.bfloat16)
        out_low = (out - out_high.astype(jnp.float32)).astype(jnp.bfloat16)
        left_high[:, piece, :] = out_high.reshape(width, ROWS, blk)
        left_low[:, piece, :] = out_low.reshape(width, ROWS, blk)
        return carry

    lax.fori_loop(0, blk // ROWS, mix_rows, 0)

    def apply_left(u, carry):
        out = jnp.dot(left_high[u], live_wide, preferred_element_type=jnp.float32) + jnp.dot(
            left_low[u], live_wide, preferred_element_type=jnp.float32
        )
        out = out.astype(jnp.bfloat16)
        for v in range(count):
            mixed[u, pl.ds(v * blk, blk), :] = out[:, v * blk : (v + 1) * blk]
        return carry

    lax.fori_loop(0, width, apply_left, 0)

    total[...] = jnp.zeros_like(total)

    @pl.when(has_partner)
    def _():
        def apply_right(i, carry):
            env_copy(i).wait_recv()
            out = total[...]
            for j in range(group):
                u = i * group + j
                out += lax.dot_general(
                    mixed[u],
                    arrived[u],
                    (((1,), (1,)), ((), ())),
                    preferred_element_type=jnp.float32,
                )
            total[...] = out
            return carry

        lax.fori_loop(0, steps, apply_right, 0)

    terms[...] = jnp.zeros_like(terms)
    lanes = terms.shape[1]
    for j in range(count):
        block = jnp.where(mask, total[pl.ds(j * blk, blk), :], 0.0).astype(jnp.bfloat16)
        product[j, 0] = block
        block = block.astype(jnp.float32)
        for i in range(count):
            line = jnp.sum(live[i].astype(jnp.float32) * block, axis=0, keepdims=True)
            short = line[:, :lanes]
            for part in range(1, blk // lanes):
                short = short + line[:, part * lanes : (part + 1) * lanes]
            row = i * count + j
            terms[row : row + 1, :] = short

    gathered[here] = terms[...]

    def term_copy(k):
        return pltpu.make_async_remote_copy(
            src_ref=terms,
            dst_ref=gathered.at[here],
            send_sem=term_send_sem.at[k],
            recv_sem=term_recv_sem.at[k],
            device_id={"sector": lax.rem(here + k, sectors)},
            device_id_type=MESH,
        )

    def send_terms(k, carry):
        term_copy(k).start()
        return carry

    def wait_terms(k, carry):
        term_copy(k).wait_recv()
        return carry

    def wait_terms_sent(k, carry):
        term_copy(k).wait_send()
        return carry

    lax.fori_loop(1, sectors, send_terms, 0)
    lax.fori_loop(1, sectors, wait_terms, 0)

    summed = gathered[0]
    for s in range(1, sectors):
        summed = summed + gathered[s]
    scale = 1.0 / jnp.sqrt(jnp.float32(sectors * blk * blk))
    sums = jnp.sum(summed, axis=1, keepdims=True) * scale
    out_rows = lax.broadcasted_iota(jnp.int32, (count, count), 0)
    out_cols = lax.broadcasted_iota(jnp.int32, (count, count), 1)
    result = jnp.zeros((count, count), jnp.float32)
    for i in range(count):
        for j in range(count):
            row = i * count + j
            value = jnp.broadcast_to(sums[row : row + 1, :], (count, count))
            result = jnp.where((out_rows == i) & (out_cols == j), value, result)
    subspace[...] = result

    lax.fori_loop(1, sectors, wait_terms_sent, 0)

    @pl.when(here > 0)
    def _():
        def sent(i, carry):
            env_copy(i).wait_send()
            return carry

        lax.fori_loop(0, steps, sent, 0)


def shards(
    vectors, left_environment_blocks, right_env, mpo_coef, mpo_pattern, left_sizes, right_sizes
):
    count, _, blk, _ = vectors.shape
    width = left_environment_blocks.shape[1]
    sectors = lax.axis_size("sector")
    group = 2 if width % 2 == 0 else 1
    steps = width // group
    tile_rows = -(-count * count // 8) * 8
    vmem = pl.BlockSpec(memory_space=pltpu.VMEM)
    smem = pl.BlockSpec(memory_space=pltpu.SMEM)
    hbm = pl.BlockSpec(memory_space=pl.ANY)
    return pl.pallas_call(
        functools.partial(kernel, sectors, group),
        out_shape=(
            jax.ShapeDtypeStruct(vectors.shape, jnp.bfloat16),
            jax.ShapeDtypeStruct((count, count), jnp.float32),
        ),
        in_specs=[smem, smem, vmem, vmem, vmem, hbm, hbm],
        out_specs=(vmem, vmem),
        scratch_shapes=[
            pltpu.VMEM((width, blk, blk), jnp.bfloat16),
            pltpu.VMEM((width, blk, blk), jnp.bfloat16),
            pltpu.VMEM((width, blk, blk), jnp.bfloat16),
            pltpu.VMEM((width, count * blk, blk), jnp.bfloat16),
            pltpu.VMEM((width, blk, blk), jnp.bfloat16),
            pltpu.VMEM((count * blk, blk), jnp.float32),
            pltpu.VMEM((tile_rows, 128), jnp.float32),
            pltpu.VMEM((sectors, tile_rows, 128), jnp.float32),
            pltpu.SemaphoreType.DMA,
            pltpu.SemaphoreType.DMA((steps,)),
            pltpu.SemaphoreType.DMA((steps,)),
            pltpu.SemaphoreType.DMA((sectors,)),
            pltpu.SemaphoreType.DMA((sectors,)),
        ],
        compiler_params=pltpu.CompilerParams(
            collective_id=0, has_side_effects=True, vmem_limit_bytes=48 * 1024 * 1024
        ),
        cost_estimate=pl.CostEstimate(
            flops=4 * width * blk * blk * blk * count,
            bytes_accessed=3 * width * blk * blk * 2,
            transcendentals=0,
        ),
    )(
        left_sizes,
        right_sizes,
        mpo_coef,
        mpo_pattern,
        vectors,
        left_environment_blocks,
        right_env,
    )


def solution(mesh):
    placed = (
        P(None, ("parts", "sector"), None, None),
        P(("parts", "sector"), None, None, None),
        P(("parts", "sector"), None, None, None),
        P("parts", None),
        P("parts", None),
        P("parts"),
        P("parts"),
    )
    return jax.shard_map(
        shards,
        mesh=mesh,
        in_specs=placed,
        out_specs=(P(None, ("parts", "sector"), None, None), P("parts", None)),
        check_vma=False,
    )
```

```python
import functools

import jax
import jax.numpy as jnp
from jax import lax
from jax.experimental import pallas as pl
from jax.experimental.pallas import tpu as pltpu
from jax.sharding import PartitionSpec as P

MESH = pl.DeviceIdType.MESH
ROWS = 16


def kernel(
    sectors,
    group,
    left_sizes_in,
    right_sizes_in,
    coef_in,
    pattern_in,
    vectors_in,
    left_env,
    right_env,
    product,
    subspace,
    left_sizes,
    right_sizes,
    coef,
    pattern,
    vectors,
    left,
    left_high,
    left_low,
    mixed,
    arrived,
    total,
    terms,
    gathered,
    small_sem,
    left_sem,
    send_sem,
    recv_sem,
    term_send_sem,
    term_recv_sem,
):
    count, _, blk, _ = vectors.shape
    width = coef.shape[0]
    steps = width // group
    wide = width * ROWS
    here = lax.axis_index("sector")
    has_partner = here + 1 < sectors

    barrier = pltpu.get_barrier_semaphore()

    def greet(k, carry):
        peer = lax.rem(here + k, sectors)
        pl.semaphore_signal(barrier, inc=1, device_id={"sector": peer}, device_id_type=MESH)
        return carry

    lax.fori_loop(1, sectors, greet, 0)

    left_copy = pltpu.make_async_copy(left_env.at[0], left, left_sem)
    small = (
        (left_sizes_in, left_sizes),
        (right_sizes_in, right_sizes),
        (coef_in, coef),
        (pattern_in, pattern),
        (vectors_in, vectors),
    )
    small_copies = [
        pltpu.make_async_copy(src, dst, small_sem.at[i]) for i, (src, dst) in enumerate(small)
    ]
    for copy in small_copies:
        copy.start()
    left_copy.start()
    pl.semaphore_wait(barrier, sectors - 1)

    def env_copy(i):
        piece = pl.ds(i * group, group)
        return pltpu.make_async_remote_copy(
            src_ref=right_env.at[0, piece],
            dst_ref=arrived.at[piece],
            send_sem=send_sem.at[i],
            recv_sem=recv_sem.at[i],
            device_id={"sector": lax.rem(here + sectors - 1, sectors)},
            device_id_type=MESH,
        )

    @pl.when(here > 0)
    def _():
        def send(i, carry):
            env_copy(i).start()
            return carry

        lax.fori_loop(0, steps, send, 0)

    for copy in small_copies:
        copy.wait()

    partner = jnp.minimum(here + 1, sectors - 1)
    row_limit = left_sizes[here]
    col_limit = jnp.where(has_partner, right_sizes[partner], 0)
    rows = lax.broadcasted_iota(jnp.int32, (blk, blk), 0)
    cols = lax.broadcasted_iota(jnp.int32, (blk, blk), 1)
    mask = (rows < row_limit) & (cols < col_limit)
    live = [
        jnp.where(mask, vectors[v, 0].astype(jnp.float32), 0.0).astype(jnp.bfloat16)
        for v in range(count)
    ]
    live_wide = jnp.concatenate(live, axis=1)

    coupling = coef[...] * pattern[...].astype(jnp.float32)
    high = coupling.astype(jnp.bfloat16)
    low = (coupling - high.astype(jnp.float32)).astype(jnp.bfloat16)
    pick_rows = (
        lax.broadcasted_iota(jnp.int32, (wide, width), 0) // ROWS
        == lax.broadcasted_iota(jnp.int32, (wide, width), 1)
    ).astype(jnp.float32).astype(jnp.bfloat16)
    pick_cols = (
        lax.broadcasted_iota(jnp.int32, (width, wide), 1) // ROWS
        == lax.broadcasted_iota(jnp.int32, (width, wide), 0)
    ).astype(jnp.float32).astype(jnp.bfloat16)
    same = (
        lax.broadcasted_iota(jnp.int32, (wide, wide), 0) % ROWS
        == lax.broadcasted_iota(jnp.int32, (wide, wide), 1) % ROWS
    )

    def spread(part):
        tall = lax.dot_general(
            pick_rows, part, (((1,), (1,)), ((), ())), preferred_element_type=jnp.float32
        ).astype(jnp.bfloat16)
        full = jnp.dot(tall, pick_cols, preferred_element_type=jnp.float32)
        return jnp.where(same, full, 0.0).astype(jnp.bfloat16)

    spread_high = spread(high)
    spread_low = spread(low)

    left_copy.wait()

    def mix_rows(g, carry):
        piece = pl.ds(pl.multiple_of(g * ROWS, ROWS), ROWS)
        block = left[:, piece, :].reshape(wide, blk)
        out = jnp.dot(spread_high, block, preferred_element_type=jnp.float32) + jnp.dot(
            spread_low, block, preferred_element_type=jnp.float32
        )
        out_high = out.astype(jnp.bfloat16)
        out_low = (out - out_high.astype(jnp.float32)).astype(jnp.bfloat16)
        left_high[:, piece, :] = out_high.reshape(width, ROWS, blk)
        left_low[:, piece, :] = out_low.reshape(width, ROWS, blk)
        return carry

    lax.fori_loop(0, blk // ROWS, mix_rows, 0)

    def apply_left(u, carry):
        out = jnp.dot(left_high[u], live_wide, preferred_element_type=jnp.float32) + jnp.dot(
            left_low[u], live_wide, preferred_element_type=jnp.float32
        )
        out = out.astype(jnp.bfloat16)
        for v in range(count):
            mixed[u, pl.ds(v * blk, blk), :] = out[:, v * blk : (v + 1) * blk]
        return carry

    lax.fori_loop(0, width, apply_left, 0)

    total[...] = jnp.zeros_like(total)

    @pl.when(has_partner)
    def _():
        def apply_right(i, carry):
            env_copy(i).wait_recv()
            out = total[...]
            for j in range(group):
                u = i * group + j
                out += lax.dot_general(
                    mixed[u],
                    arrived[u],
                    (((1,), (1,)), ((), ())),
                    preferred_element_type=jnp.float32,
                )
            total[...] = out
            return carry

        lax.fori_loop(0, steps, apply_right, 0)

    terms[...] = jnp.zeros_like(terms)
    lanes = terms.shape[1]
    for j in range(count):
        block = jnp.where(mask, total[pl.ds(j * blk, blk), :], 0.0).astype(jnp.bfloat16)
        product[j, 0] = block
        block = block.astype(jnp.float32)
        for i in range(count):
            line = jnp.sum(live[i].astype(jnp.float32) * block, axis=0, keepdims=True)
            short = line[:, :lanes]
            for part in range(1, blk // lanes):
                short = short + line[:, part * lanes : (part + 1) * lanes]
            row = i * count + j
            terms[row : row + 1, :] = short

    gathered[here] = terms[...]

    def term_copy(k):
        return pltpu.make_async_remote_copy(
            src_ref=terms,
            dst_ref=gathered.at[here],
            send_sem=term_send_sem.at[k],
            recv_sem=term_recv_sem.at[k],
            device_id={"sector": lax.rem(here + k, sectors)},
            device_id_type=MESH,
        )

    def send_terms(k, carry):
        term_copy(k).start()
        return carry

    def wait_terms(k, carry):
        term_copy(k).wait_recv()
        return carry

    def wait_terms_sent(k, carry):
        term_copy(k).wait_send()
        return carry

    lax.fori_loop(1, sectors, send_terms, 0)
    lax.fori_loop(1, sectors, wait_terms, 0)

    summed = gathered[0]
    for s in range(1, sectors):
        summed = summed + gathered[s]
    scale = 1.0 / jnp.sqrt(jnp.float32(sectors * blk * blk))
    sums = jnp.sum(summed, axis=1, keepdims=True) * scale
    out_rows = lax.broadcasted_iota(jnp.int32, (count, count), 0)
    out_cols = lax.broadcasted_iota(jnp.int32, (count, count), 1)
    result = jnp.zeros((count, count), jnp.float32)
    for i in range(count):
        for j in range(count):
            row = i * count + j
            value = jnp.broadcast_to(sums[row : row + 1, :], (count, count))
            result = jnp.where((out_rows == i) & (out_cols == j), value, result)
    subspace[...] = result

    lax.fori_loop(1, sectors, wait_terms_sent, 0)

    @pl.when(here > 0)
    def _():
        def sent(i, carry):
            env_copy(i).wait_send()
            return carry

        lax.fori_loop(0, steps, sent, 0)


def shards(
    vectors, left_environment_blocks, right_env, mpo_coef, mpo_pattern, left_sizes, right_sizes
):
    count, _, blk, _ = vectors.shape
    width = left_environment_blocks.shape[1]
    sectors = lax.axis_size("sector")
    group = 2 if width % 2 == 0 else 1
    steps = width // group
    tile_rows = -(-count * count // 8) * 8
    vmem = pl.BlockSpec(memory_space=pltpu.VMEM)
    hbm = pl.BlockSpec(memory_space=pltpu.HBM)
    return pl.pallas_call(
        functools.partial(kernel, sectors, group),
        out_shape=(
            jax.ShapeDtypeStruct(vectors.shape, jnp.bfloat16),
            jax.ShapeDtypeStruct((count, count), jnp.float32),
        ),
        in_specs=[hbm] * 7,
        out_specs=(vmem, vmem),
        scratch_shapes=[
            pltpu.SMEM(left_sizes.shape, jnp.int32),
            pltpu.SMEM(right_sizes.shape, jnp.int32),
            pltpu.VMEM(mpo_coef.shape, jnp.float32),
            pltpu.VMEM(mpo_pattern.shape, jnp.int32),
            pltpu.VMEM(vectors.shape, jnp.bfloat16),
            pltpu.VMEM((width, blk, blk), jnp.bfloat16),
            pltpu.VMEM((width, blk, blk), jnp.bfloat16),
            pltpu.VMEM((width, blk, blk), jnp.bfloat16),
            pltpu.VMEM((width, count * blk, blk), jnp.bfloat16),
            pltpu.VMEM((width, blk, blk), jnp.bfloat16),
            pltpu.VMEM((count * blk, blk), jnp.float32),
            pltpu.VMEM((tile_rows, 128), jnp.float32),
            pltpu.VMEM((sectors, tile_rows, 128), jnp.float32),
            pltpu.SemaphoreType.DMA((5,)),
            pltpu.SemaphoreType.DMA,
            pltpu.SemaphoreType.DMA((steps,)),
            pltpu.SemaphoreType.DMA((steps,)),
            pltpu.SemaphoreType.DMA((sectors,)),
            pltpu.SemaphoreType.DMA((sectors,)),
        ],
        compiler_params=pltpu.CompilerParams(
            collective_id=0, has_side_effects=True, vmem_limit_bytes=48 * 1024 * 1024
        ),
        cost_estimate=pl.CostEstimate(
            flops=4 * width * blk * blk * blk * count,
            bytes_accessed=3 * width * blk * blk * 2,
            transcendentals=0,
        ),
    )(
        left_sizes,
        right_sizes,
        mpo_coef,
        mpo_pattern,
        vectors,
        left_environment_blocks,
        right_env,
    )


def solution(mesh):
    placed = (
        P(None, ("parts", "sector"), None, None),
        P(("parts", "sector"), None, None, None),
        P(("parts", "sector"), None, None, None),
        P("parts", None),
        P("parts", None),
        P("parts"),
        P("parts"),
    )
    return jax.shard_map(
        shards,
        mesh=mesh,
        in_specs=placed,
        out_specs=(P(None, ("parts", "sector"), None, None), P("parts", None)),
        check_vma=False,
    )
```

```python
import functools

import jax
import jax.numpy as jnp
from jax import lax
from jax.experimental import pallas as pl
from jax.experimental.pallas import tpu as pltpu
from jax.sharding import PartitionSpec as P

MESH = pl.DeviceIdType.MESH
ROWS = 16


def kernel(
    sectors,
    group,
    left_sizes_in,
    right_sizes_in,
    coef_in,
    pattern_in,
    vectors_in,
    left_env,
    right_env,
    product,
    subspace,
    left_sizes,
    right_sizes,
    coef,
    pattern,
    vectors,
    result_block,
    left,
    left_high,
    left_low,
    mixed,
    arrived,
    total,
    terms,
    gathered,
    small_sem,
    left_sem,
    send_sem,
    recv_sem,
    term_send_sem,
    term_recv_sem,
):
    count, _, blk, _ = vectors.shape
    width = coef.shape[0]
    steps = width // group
    wide = width * ROWS
    here = lax.axis_index("sector")
    has_partner = here + 1 < sectors

    barrier = pltpu.get_barrier_semaphore()

    def greet(k, carry):
        peer = lax.rem(here + k, sectors)
        pl.semaphore_signal(barrier, inc=1, device_id={"sector": peer}, device_id_type=MESH)
        return carry

    lax.fori_loop(1, sectors, greet, 0)

    left_copy = pltpu.make_async_copy(left_env.at[0], left, left_sem)
    small = (
        (left_sizes_in, left_sizes),
        (right_sizes_in, right_sizes),
        (coef_in, coef),
        (pattern_in, pattern),
        (vectors_in, vectors),
    )
    small_copies = [
        pltpu.make_async_copy(src, dst, small_sem.at[i]) for i, (src, dst) in enumerate(small)
    ]
    for copy in small_copies:
        copy.start()
    left_copy.start()
    pl.semaphore_wait(barrier, sectors - 1)

    def env_copy(i):
        piece = pl.ds(i * group, group)
        return pltpu.make_async_remote_copy(
            src_ref=right_env.at[0, piece],
            dst_ref=arrived.at[piece],
            send_sem=send_sem.at[i],
            recv_sem=recv_sem.at[i],
            device_id={"sector": lax.rem(here + sectors - 1, sectors)},
            device_id_type=MESH,
        )

    @pl.when(here > 0)
    def _():
        def send(i, carry):
            env_copy(i).start()
            return carry

        lax.fori_loop(0, steps, send, 0)

    for copy in small_copies:
        copy.wait()

    partner = jnp.minimum(here + 1, sectors - 1)
    row_limit = left_sizes[here]
    col_limit = jnp.where(has_partner, right_sizes[partner], 0)
    rows = lax.broadcasted_iota(jnp.int32, (blk, blk), 0)
    cols = lax.broadcasted_iota(jnp.int32, (blk, blk), 1)
    mask = (rows < row_limit) & (cols < col_limit)
    live = [
        jnp.where(mask, vectors[v, 0].astype(jnp.float32), 0.0).astype(jnp.bfloat16)
        for v in range(count)
    ]
    live_wide = jnp.concatenate(live, axis=1)

    coupling = coef[...] * pattern[...].astype(jnp.float32)
    high = coupling.astype(jnp.bfloat16)
    low = (coupling - high.astype(jnp.float32)).astype(jnp.bfloat16)
    pick_rows = (
        lax.broadcasted_iota(jnp.int32, (wide, width), 0) // ROWS
        == lax.broadcasted_iota(jnp.int32, (wide, width), 1)
    ).astype(jnp.float32).astype(jnp.bfloat16)
    pick_cols = (
        lax.broadcasted_iota(jnp.int32, (width, wide), 1) // ROWS
        == lax.broadcasted_iota(jnp.int32, (width, wide), 0)
    ).astype(jnp.float32).astype(jnp.bfloat16)
    same = (
        lax.broadcasted_iota(jnp.int32, (wide, wide), 0) % ROWS
        == lax.broadcasted_iota(jnp.int32, (wide, wide), 1) % ROWS
    )

    def spread(part):
        tall = lax.dot_general(
            pick_rows, part, (((1,), (1,)), ((), ())), preferred_element_type=jnp.float32
        ).astype(jnp.bfloat16)
        full = jnp.dot(tall, pick_cols, preferred_element_type=jnp.float32)
        return jnp.where(same, full, 0.0).astype(jnp.bfloat16)

    spread_high = spread(high)
    spread_low = spread(low)

    left_copy.wait()

    def mix_rows(g, carry):
        piece = pl.ds(pl.multiple_of(g * ROWS, ROWS), ROWS)
        block = left[:, piece, :].reshape(wide, blk)
        out = jnp.dot(spread_high, block, preferred_element_type=jnp.float32) + jnp.dot(
            spread_low, block, preferred_element_type=jnp.float32
        )
        out_high = out.astype(jnp.bfloat16)
        out_low = (out - out_high.astype(jnp.float32)).astype(jnp.bfloat16)
        left_high[:, piece, :] = out_high.reshape(width, ROWS, blk)
        left_low[:, piece, :] = out_low.reshape(width, ROWS, blk)
        return carry

    lax.fori_loop(0, blk // ROWS, mix_rows, 0)

    def apply_left(u, carry):
        out = jnp.dot(left_high[u], live_wide, preferred_element_type=jnp.float32) + jnp.dot(
            left_low[u], live_wide, preferred_element_type=jnp.float32
        )
        out = out.astype(jnp.bfloat16)
        for v in range(count):
            mixed[u, pl.ds(v * blk, blk), :] = out[:, v * blk : (v + 1) * blk]
        return carry

    lax.fori_loop(0, width, apply_left, 0)

    total[...] = jnp.zeros_like(total)

    @pl.when(has_partner)
    def _():
        def apply_right(i, carry):
            env_copy(i).wait_recv()
            out = total[...]
            for j in range(group):
                u = i * group + j
                out += lax.dot_general(
                    mixed[u],
                    arrived[u],
                    (((1,), (1,)), ((), ())),
                    preferred_element_type=jnp.float32,
                )
            total[...] = out
            return carry

        lax.fori_loop(0, steps, apply_right, 0)

    terms[...] = jnp.zeros_like(terms)
    lanes = terms.shape[1]
    blocks = [
        jnp.where(mask, total[pl.ds(j * blk, blk), :], 0.0).astype(jnp.bfloat16)
        for j in range(count)
    ]
    for j in range(count):
        block = blocks[j].astype(jnp.float32)
        for i in range(count):
            line = jnp.sum(live[i].astype(jnp.float32) * block, axis=0, keepdims=True)
            short = line[:, :lanes]
            for part in range(1, blk // lanes):
                short = short + line[:, part * lanes : (part + 1) * lanes]
            row = i * count + j
            terms[row : row + 1, :] = short

    def term_copy(k):
        return pltpu.make_async_remote_copy(
            src_ref=terms,
            dst_ref=gathered.at[here],
            send_sem=term_send_sem.at[k],
            recv_sem=term_recv_sem.at[k],
            device_id={"sector": lax.rem(here + k, sectors)},
            device_id_type=MESH,
        )

    def send_terms(k, carry):
        term_copy(k).start()
        return carry

    def wait_terms(k, carry):
        term_copy(k).wait_recv()
        return carry

    def wait_terms_sent(k, carry):
        term_copy(k).wait_send()
        return carry

    lax.fori_loop(1, sectors, send_terms, 0)
    gathered[here] = terms[...]
    for j in range(count):
        result_block[j, 0] = blocks[j]
    product_copy = pltpu.make_async_copy(result_block, product, left_sem)
    product_copy.start()
    lax.fori_loop(1, sectors, wait_terms, 0)

    summed = gathered[0]
    for s in range(1, sectors):
        summed = summed + gathered[s]
    scale = 1.0 / jnp.sqrt(jnp.float32(sectors * blk * blk))
    sums = jnp.sum(summed, axis=1, keepdims=True) * scale
    out_rows = lax.broadcasted_iota(jnp.int32, (count, count), 0)
    out_cols = lax.broadcasted_iota(jnp.int32, (count, count), 1)
    result = jnp.zeros((count, count), jnp.float32)
    for i in range(count):
        for j in range(count):
            row = i * count + j
            value = jnp.broadcast_to(sums[row : row + 1, :], (count, count))
            result = jnp.where((out_rows == i) & (out_cols == j), value, result)
    subspace[...] = result
    product_copy.wait()

    lax.fori_loop(1, sectors, wait_terms_sent, 0)

    @pl.when(here > 0)
    def _():
        def sent(i, carry):
            env_copy(i).wait_send()
            return carry

        lax.fori_loop(0, steps, sent, 0)


def finish(product_in, subspace_in, product, subspace, sem):
    first = pltpu.make_async_copy(product_in, product, sem.at[0])
    second = pltpu.make_async_copy(subspace_in, subspace, sem.at[1])
    first.start()
    second.start()
    first.wait()
    second.wait()


def shards(
    vectors, left_environment_blocks, right_env, mpo_coef, mpo_pattern, left_sizes, right_sizes
):
    count, _, blk, _ = vectors.shape
    width = left_environment_blocks.shape[1]
    sectors = lax.axis_size("sector")
    group = 2 if width % 2 == 0 else 1
    steps = width // group
    tile_rows = -(-count * count // 8) * 8
    vmem = pl.BlockSpec(memory_space=pltpu.VMEM)
    hbm = pl.BlockSpec(memory_space=pltpu.HBM)
    product, subspace = pl.pallas_call(
        functools.partial(kernel, sectors, group),
        out_shape=(
            jax.ShapeDtypeStruct(vectors.shape, jnp.bfloat16),
            jax.ShapeDtypeStruct((count, count), jnp.float32),
        ),
        in_specs=[hbm] * 7,
        out_specs=(hbm, vmem),
        scratch_shapes=[
            pltpu.SMEM(left_sizes.shape, jnp.int32),
            pltpu.SMEM(right_sizes.shape, jnp.int32),
            pltpu.VMEM(mpo_coef.shape, jnp.float32),
            pltpu.VMEM(mpo_pattern.shape, jnp.int32),
            pltpu.VMEM(vectors.shape, jnp.bfloat16),
            pltpu.VMEM(vectors.shape, jnp.bfloat16),
            pltpu.VMEM((width, blk, blk), jnp.bfloat16),
            pltpu.VMEM((width, blk, blk), jnp.bfloat16),
            pltpu.VMEM((width, blk, blk), jnp.bfloat16),
            pltpu.VMEM((width, count * blk, blk), jnp.bfloat16),
            pltpu.VMEM((width, blk, blk), jnp.bfloat16),
            pltpu.VMEM((count * blk, blk), jnp.float32),
            pltpu.VMEM((tile_rows, 128), jnp.float32),
            pltpu.VMEM((sectors, tile_rows, 128), jnp.float32),
            pltpu.SemaphoreType.DMA((5,)),
            pltpu.SemaphoreType.DMA,
            pltpu.SemaphoreType.DMA((steps,)),
            pltpu.SemaphoreType.DMA((steps,)),
            pltpu.SemaphoreType.DMA((sectors,)),
            pltpu.SemaphoreType.DMA((sectors,)),
        ],
        compiler_params=pltpu.CompilerParams(
            collective_id=0, has_side_effects=True, vmem_limit_bytes=60 * 1024 * 1024
        ),
        cost_estimate=pl.CostEstimate(
            flops=4 * width * blk * blk * blk * count,
            bytes_accessed=3 * width * blk * blk * 2,
            transcendentals=0,
        ),
    )(
        left_sizes,
        right_sizes,
        mpo_coef,
        mpo_pattern,
        vectors,
        left_environment_blocks,
        right_env,
    )
    return pl.pallas_call(
        finish,
        out_shape=(
            jax.ShapeDtypeStruct(product.shape, product.dtype),
            jax.ShapeDtypeStruct(subspace.shape, subspace.dtype),
        ),
        in_specs=[vmem, vmem],
        out_specs=(hbm, hbm),
        scratch_shapes=[pltpu.SemaphoreType.DMA((2,))],
    )(product, subspace)


def solution(mesh):
    placed = (
        P(None, ("parts", "sector"), None, None),
        P(("parts", "sector"), None, None, None),
        P(("parts", "sector"), None, None, None),
        P("parts", None),
        P("parts", None),
        P("parts"),
        P("parts"),
    )
    return jax.shard_map(
        shards,
        mesh=mesh,
        in_specs=placed,
        out_specs=(P(None, ("parts", "sector"), None, None), P("parts", None)),
        check_vma=False,
    )
```

```python
import functools

import jax
import jax.numpy as jnp
from jax import lax
from jax.experimental import pallas as pl
from jax.experimental.pallas import tpu as pltpu
from jax.sharding import PartitionSpec as P

MESH = pl.DeviceIdType.MESH
ROWS = 16


def kernel(
    sectors,
    group,
    left_sizes_in,
    right_sizes_in,
    coef_in,
    pattern_in,
    vectors_in,
    left_env,
    right_env,
    product,
    subspace,
    left_sizes,
    right_sizes,
    coef,
    pattern,
    vectors,
    result_block,
    left,
    left_high,
    left_low,
    mixed,
    arrived,
    total,
    terms,
    gathered,
    small_sem,
    left_sem,
    send_sem,
    recv_sem,
    term_send_sem,
    term_recv_sem,
):
    count, _, blk, _ = vectors.shape
    width = coef.shape[0]
    wide = width * ROWS
    here = lax.axis_index("sector")
    has_partner = here + 1 < sectors

    barrier = pltpu.get_barrier_semaphore()

    def greet(k, carry):
        peer = lax.rem(here + k, sectors)
        pl.semaphore_signal(barrier, inc=1, device_id={"sector": peer}, device_id_type=MESH)
        return carry

    lax.fori_loop(1, sectors, greet, 0)

    left_copy = pltpu.make_async_copy(left_env.at[0], left, left_sem)
    small = (
        (left_sizes_in, left_sizes),
        (right_sizes_in, right_sizes),
        (coef_in, coef),
        (pattern_in, pattern),
        (vectors_in, vectors),
    )
    small_copies = [
        pltpu.make_async_copy(src, dst, small_sem.at[i]) for i, (src, dst) in enumerate(small)
    ]
    for copy in small_copies:
        copy.start()
    left_copy.start()
    pl.semaphore_wait(barrier, sectors - 1)

    def env_copy(i):
        piece = pl.ds(*group[i])
        return pltpu.make_async_remote_copy(
            src_ref=right_env.at[0, piece],
            dst_ref=arrived.at[piece],
            send_sem=send_sem.at[i],
            recv_sem=recv_sem.at[i],
            device_id={"sector": lax.rem(here + sectors - 1, sectors)},
            device_id_type=MESH,
        )

    @pl.when(here > 0)
    def _():
        for i in range(len(group)):
            env_copy(i).start()

    for copy in small_copies:
        copy.wait()

    partner = jnp.minimum(here + 1, sectors - 1)
    row_limit = left_sizes[here]
    col_limit = jnp.where(has_partner, right_sizes[partner], 0)
    rows = lax.broadcasted_iota(jnp.int32, (blk, blk), 0)
    cols = lax.broadcasted_iota(jnp.int32, (blk, blk), 1)
    mask = (rows < row_limit) & (cols < col_limit)
    live = [
        jnp.where(mask, vectors[v, 0].astype(jnp.float32), 0.0).astype(jnp.bfloat16)
        for v in range(count)
    ]
    live_wide = jnp.concatenate(live, axis=1)

    coupling = coef[...] * pattern[...].astype(jnp.float32)
    high = coupling.astype(jnp.bfloat16)
    low = (coupling - high.astype(jnp.float32)).astype(jnp.bfloat16)
    pick_rows = (
        lax.broadcasted_iota(jnp.int32, (wide, width), 0) // ROWS
        == lax.broadcasted_iota(jnp.int32, (wide, width), 1)
    ).astype(jnp.float32).astype(jnp.bfloat16)
    pick_cols = (
        lax.broadcasted_iota(jnp.int32, (width, wide), 1) // ROWS
        == lax.broadcasted_iota(jnp.int32, (width, wide), 0)
    ).astype(jnp.float32).astype(jnp.bfloat16)
    same = (
        lax.broadcasted_iota(jnp.int32, (wide, wide), 0) % ROWS
        == lax.broadcasted_iota(jnp.int32, (wide, wide), 1) % ROWS
    )

    def spread(part):
        tall = lax.dot_general(
            pick_rows, part, (((1,), (1,)), ((), ())), preferred_element_type=jnp.float32
        ).astype(jnp.bfloat16)
        full = jnp.dot(tall, pick_cols, preferred_element_type=jnp.float32)
        return jnp.where(same, full, 0.0).astype(jnp.bfloat16)

    spread_high = spread(high)
    spread_low = spread(low)

    left_copy.wait()

    def mix_rows(g, carry):
        piece = pl.ds(pl.multiple_of(g * ROWS, ROWS), ROWS)
        block = left[:, piece, :].reshape(wide, blk)
        out = jnp.dot(spread_high, block, preferred_element_type=jnp.float32) + jnp.dot(
            spread_low, block, preferred_element_type=jnp.float32
        )
        out_high = out.astype(jnp.bfloat16)
        out_low = (out - out_high.astype(jnp.float32)).astype(jnp.bfloat16)
        left_high[:, piece, :] = out_high.reshape(width, ROWS, blk)
        left_low[:, piece, :] = out_low.reshape(width, ROWS, blk)
        return carry

    lax.fori_loop(0, blk // ROWS, mix_rows, 0)

    def apply_left(u, carry):
        out = jnp.dot(left_high[u], live_wide, preferred_element_type=jnp.float32) + jnp.dot(
            left_low[u], live_wide, preferred_element_type=jnp.float32
        )
        out = out.astype(jnp.bfloat16)
        for v in range(count):
            mixed[u, pl.ds(v * blk, blk), :] = out[:, v * blk : (v + 1) * blk]
        return carry

    lax.fori_loop(0, width, apply_left, 0)

    total[...] = jnp.zeros_like(total)

    @pl.when(has_partner)
    def _():
        def apply_right(u, carry):
            total[...] += lax.dot_general(
                mixed[u], arrived[u], (((1,), (1,)), ((), ())), preferred_element_type=jnp.float32
            )
            return carry

        for i, (first, size) in enumerate(group):
            env_copy(i).wait_recv()
            lax.fori_loop(first, first + size, apply_right, 0)

    terms[...] = jnp.zeros_like(terms)
    lanes = terms.shape[1]
    blocks = [
        jnp.where(mask, total[pl.ds(j * blk, blk), :], 0.0).astype(jnp.bfloat16)
        for j in range(count)
    ]
    for j in range(count):
        block = blocks[j].astype(jnp.float32)
        for i in range(count):
            line = jnp.sum(live[i].astype(jnp.float32) * block, axis=0, keepdims=True)
            short = line[:, :lanes]
            for part in range(1, blk // lanes):
                short = short + line[:, part * lanes : (part + 1) * lanes]
            row = i * count + j
            terms[row : row + 1, :] = short

    def term_copy(k):
        return pltpu.make_async_remote_copy(
            src_ref=terms,
            dst_ref=gathered.at[here],
            send_sem=term_send_sem.at[k],
            recv_sem=term_recv_sem.at[k],
            device_id={"sector": lax.rem(here + k, sectors)},
            device_id_type=MESH,
        )

    def send_terms(k, carry):
        term_copy(k).start()
        return carry

    def wait_terms(k, carry):
        term_copy(k).wait_recv()
        return carry

    def wait_terms_sent(k, carry):
        term_copy(k).wait_send()
        return carry

    lax.fori_loop(1, sectors, send_terms, 0)
    gathered[here] = terms[...]
    for j in range(count):
        result_block[j, 0] = blocks[j]
    product_copy = pltpu.make_async_copy(result_block, product, left_sem)
    product_copy.start()
    lax.fori_loop(1, sectors, wait_terms, 0)

    summed = gathered[0]
    for s in range(1, sectors):
        summed = summed + gathered[s]
    scale = 1.0 / jnp.sqrt(jnp.float32(sectors * blk * blk))
    sums = jnp.sum(summed, axis=1, keepdims=True) * scale
    out_rows = lax.broadcasted_iota(jnp.int32, (count, count), 0)
    out_cols = lax.broadcasted_iota(jnp.int32, (count, count), 1)
    result = jnp.zeros((count, count), jnp.float32)
    for i in range(count):
        for j in range(count):
            row = i * count + j
            value = jnp.broadcast_to(sums[row : row + 1, :], (count, count))
            result = jnp.where((out_rows == i) & (out_cols == j), value, result)
    subspace[...] = result
    product_copy.wait()

    lax.fori_loop(1, sectors, wait_terms_sent, 0)

    @pl.when(here > 0)
    def _():
        for i in range(len(group)):
            env_copy(i).wait_send()


def finish(product_in, subspace_in, product, subspace, sem):
    first = pltpu.make_async_copy(product_in, product, sem.at[0])
    second = pltpu.make_async_copy(subspace_in, subspace, sem.at[1])
    first.start()
    second.start()
    first.wait()
    second.wait()


def shards(
    vectors, left_environment_blocks, right_env, mpo_coef, mpo_pattern, left_sizes, right_sizes
):
    count, _, blk, _ = vectors.shape
    width = left_environment_blocks.shape[1]
    sectors = lax.axis_size("sector")
    group = []
    first = 0
    while first < width:
        size = max(1, (width - first) // 2)
        group.append((first, size))
        first += size
    steps = len(group)
    tile_rows = -(-count * count // 8) * 8
    vmem = pl.BlockSpec(memory_space=pltpu.VMEM)
    hbm = pl.BlockSpec(memory_space=pltpu.HBM)
    product, subspace = pl.pallas_call(
        functools.partial(kernel, sectors, group),
        out_shape=(
            jax.ShapeDtypeStruct(vectors.shape, jnp.bfloat16),
            jax.ShapeDtypeStruct((count, count), jnp.float32),
        ),
        in_specs=[hbm] * 7,
        out_specs=(hbm, vmem),
        scratch_shapes=[
            pltpu.SMEM(left_sizes.shape, jnp.int32),
            pltpu.SMEM(right_sizes.shape, jnp.int32),
            pltpu.VMEM(mpo_coef.shape, jnp.float32),
            pltpu.VMEM(mpo_pattern.shape, jnp.int32),
            pltpu.VMEM(vectors.shape, jnp.bfloat16),
            pltpu.VMEM(vectors.shape, jnp.bfloat16),
            pltpu.VMEM((width, blk, blk), jnp.bfloat16),
            pltpu.VMEM((width, blk, blk), jnp.bfloat16),
            pltpu.VMEM((width, blk, blk), jnp.bfloat16),
            pltpu.VMEM((width, count * blk, blk), jnp.bfloat16),
            pltpu.VMEM((width, blk, blk), jnp.bfloat16),
            pltpu.VMEM((count * blk, blk), jnp.float32),
            pltpu.VMEM((tile_rows, 128), jnp.float32),
            pltpu.VMEM((sectors, tile_rows, 128), jnp.float32),
            pltpu.SemaphoreType.DMA((5,)),
            pltpu.SemaphoreType.DMA,
            pltpu.SemaphoreType.DMA((steps,)),
            pltpu.SemaphoreType.DMA((steps,)),
            pltpu.SemaphoreType.DMA((sectors,)),
            pltpu.SemaphoreType.DMA((sectors,)),
        ],
        compiler_params=pltpu.CompilerParams(
            collective_id=0, has_side_effects=True, vmem_limit_bytes=60 * 1024 * 1024
        ),
        cost_estimate=pl.CostEstimate(
            flops=4 * width * blk * blk * blk * count,
            bytes_accessed=3 * width * blk * blk * 2,
            transcendentals=0,
        ),
    )(
        left_sizes,
        right_sizes,
        mpo_coef,
        mpo_pattern,
        vectors,
        left_environment_blocks,
        right_env,
    )
    return pl.pallas_call(
        finish,
        out_shape=(
            jax.ShapeDtypeStruct(product.shape, product.dtype),
            jax.ShapeDtypeStruct(subspace.shape, subspace.dtype),
        ),
        in_specs=[vmem, vmem],
        out_specs=(hbm, hbm),
        scratch_shapes=[pltpu.SemaphoreType.DMA((2,))],
    )(product, subspace)


def solution(mesh):
    placed = (
        P(None, ("parts", "sector"), None, None),
        P(("parts", "sector"), None, None, None),
        P(("parts", "sector"), None, None, None),
        P("parts", None),
        P("parts", None),
        P("parts"),
        P("parts"),
    )
    return jax.shard_map(
        shards,
        mesh=mesh,
        in_specs=placed,
        out_specs=(P(None, ("parts", "sector"), None, None), P("parts", None)),
        check_vma=False,
    )
```
